32 devices in a mesh: groups: 2 (over y), col: 16 (over z, x, core).
Axes of the slice: x: 2, y: 2, z: 4, core: 2. Of those that a mesh axis runs over, the one named last changes fastest.
Arguments:
- base_slab: bfloat16 [8192, 53248], P('groups', 'col'), parts along dimension 0, may hold values from -6 to 6
- down_factors: bfloat16 [4096, 4096], P(('groups', 'col')), parts along dimension 0, may hold values from -6 to 6
- up_factors: bfloat16 [4096, 53248], P(('groups', 'col')), parts along dimension 0, may hold values from -0.125 to 0.125
- mix_coeffs: float32 [64], P('groups'), parts along dimension 0, may hold values from 0.2 to 2
Outputs:
- merged_slab: bfloat16 [8192, 53248], P('groups', 'col'), parts along dimension 0
The draws below stay inside these ranges and needn't reach their ends.
There are 2 independent parts, one for each index of `groups`. The reference program is written for one: setup_inputs(seed, part) draws one part's arguments, and reference() takes and returns one part's arrays. A program takes and returns all parts, laid end to end along the dimension named above; each array names one. Nothing has to cross between parts.
All inputs are finite; a program needn't handle non-finite values.
Results may differ from the reference program's by a relative error of at most 0.0038.
Values may be sent and summed in bfloat16 or wider, within the bound.
No kernel may reach another device: no remote copies, remote signals or barrier semaphores. Data moves between devices by JAX's collectives and lax.ppermute only.
A program may use at most 256 MiB of HBM per device.

```python
import math
import jax
import jax.numpy as jnp

ROWS = 4096
COLUMNS = 53248
ADAPTERS = 32
RANK = 64
TOTAL_RANK = 2048


def shard_levels(rng, extent, pieces, low, top_value):
    loudness, own = 1.0, jax.random.fold_in(rng, 6)
    for axis_at, shards_of in pieces:
        draws = jnp.exp(jax.random.uniform(jax.random.fold_in(own, axis_at), (shards_of,), jnp.float32, low / len(pieces), top_value / len(pieces)))
        loudness = loudness * jnp.repeat(draws, extent[axis_at] // shards_of).reshape([-1 if axis == axis_at else 1 for axis in range(len(extent))])
    return loudness


def scatter_about(rng, dims, spread, reach, pieces=(), kind=jnp.bfloat16):
    loudness = shard_levels(rng, dims, pieces, -0.22, 0.18) if pieces else 1.0
    result = jax.random.normal(rng, dims, jnp.float32) * spread * loudness
    return jnp.minimum(jnp.maximum(result, -reach), reach).astype(kind)


def setup_inputs(seed: int = 0, part: int = 0) -> dict:
    splits = jax.random.split(jax.random.key(seed), 5)
    part_splits = jax.random.split(jax.random.fold_in(splits[4], part), 5)
    return {
        "base_slab": scatter_about(part_splits[0], (ROWS, COLUMNS), 1.0, 6.0, ((1, 16),)),
        "down_factors": scatter_about(part_splits[1], (TOTAL_RANK, ROWS), 1.0, 6.0, ((0, 16),)),
        "up_factors": scatter_about(part_splits[2], (TOTAL_RANK, COLUMNS), TOTAL_RANK ** -0.5, 0.125, ((0, 16),)),
        "mix_coeffs": jnp.clip(jnp.exp(jax.random.uniform(part_splits[3], (ADAPTERS,), jnp.float32, math.log(0.2), math.log(2.0))), 0.2, 2.0),
    }


def reference(base_slab, down_factors, up_factors, mix_coeffs):
    per_rank = jnp.repeat(mix_coeffs.astype(jnp.float32), RANK)
    scaled = (down_factors.astype(jnp.float32) * per_rank[:, None]).astype(jnp.bfloat16)
    update = jnp.dot(scaled.T, up_factors, preferred_element_type=jnp.float32)
    return (base_slab.astype(jnp.float32) + update).astype(jnp.bfloat16)
```

```python
import functools
import jax
import jax.numpy as jnp
from jax import lax
from jax.experimental import pallas as pl
from jax.experimental.pallas import tpu as pltpu
from jax.sharding import PartitionSpec as P

RANK = 64
UNIT = 256
ORDER = (0, 1, 2, 3, 2)
VMEM = 56 * 1024 * 1024
NO_COST = pl.CostEstimate(flops=1, bytes_accessed=1, transcendentals=0)
ANY = pl.BlockSpec(memory_space=pl.ANY)


def chunk_spans(width):
    units = width // UNIT
    if width % UNIT or units < 8:
        return [(0, width)]
    sizes = [0, 0, 0, 0]
    for i in range(units):
        sizes[ORDER[i % len(ORDER)]] += UNIT
    return [(sum(sizes[:i]), s) for i, s in enumerate(sizes)]


def assemble(plan, sources, me, depth, width, offset, w, after=()):
    up = sources["up"]
    if width % 128:
        outs = []
        for blocks in plan:
            parts = []
            for b in blocks:
                if b[0] == "own":
                    parts.append(lax.dynamic_slice(up, (0, (me ^ b[1]) * width + offset), (depth, w)))
                else:
                    parts.append(sources[b[0]][b[1]][:, b[2] : b[2] + w])
            outs.append(jnp.stack(parts))
        return outs
    tile = 32 if depth % 32 == 0 else depth
    el = pl.Element
    in_specs, operands = [], []
    for blocks in plan:
        for b in blocks:
            if b[0] == "own":
                r = b[1]
                in_specs.append(pl.BlockSpec(
                    (el(tile), el(w)),
                    lambda i, m, r=r: (i * tile, pl.multiple_of((m[0] ^ r) * width + offset, 128))))
                operands.append(up)
            else:
                lead, at = b[1], b[2]
                in_specs.append(pl.BlockSpec(
                    (el(1), el(tile), el(w)), lambda i, m, lead=lead, at=at: (lead, i * tile, at)))
                operands.append(sources[b[0]])

    def kernel(m, *refs):
        ins, outs = refs[: len(operands)], refs[len(operands) + len(after) :]
        k = 0
        for blocks, out in zip(plan, outs):
            for j in range(len(blocks)):
                out[j] = ins[k][...].reshape(tile, w)
                k += 1

    return pl.pallas_call(
        kernel,
        grid_spec=pltpu.PrefetchScalarGridSpec(
            num_scalar_prefetch=1,
            grid=(depth // tile,),
            in_specs=in_specs + [ANY] * len(after),
            out_specs=[pl.BlockSpec((len(blocks), tile, w), lambda i, m: (0, i, 0)) for blocks in plan],
        ),
        out_shape=[jax.ShapeDtypeStruct((len(blocks), depth, w), up.dtype) for blocks in plan],
        compiler_params=pltpu.CompilerParams(vmem_limit_bytes=VMEM),
        cost_estimate=NO_COST,
        name="assemble",
    )(me.reshape(1), *operands, *after)


def merge(lefts, rights, me, base, out, offset, w):
    rows, width = base.shape
    depth = rights[0].shape[1]
    tile, near, groups = 512, rights[0].shape[0], len(lefts)
    n = near * groups
    if w == width:
        slab = pl.BlockSpec((tile, w), lambda i, m: (i, 0))
    else:
        slab = pl.BlockSpec((pl.Element(tile), pl.Element(w)), lambda i, m: (i * tile, offset))

    def kernel(m, *refs):
        left, right = refs[:groups], refs[groups : 2 * groups]
        base_ref, (out_ref, panel, sem) = refs[2 * groups], refs[-3:]

        @pl.when(pl.program_id(0) == 0)
        def _():
            copies = []
            for g in range(groups):
                for j in range(near):
                    place = g * near + (m[0] ^ j) % near
                    copies.append(pltpu.make_async_copy(right[g].at[j], panel.at[place], sem.at[g * near + j]))
            for c in copies:
                c.start()
            for c in copies:
                c.wait()

        update = 0.0
        for g in range(groups):
            update += lax.dot_general(
                left[g][...],
                panel[g * near : (g + 1) * near].reshape(near * depth, w),
                (((0,), (0,)), ((), ())),
                preferred_element_type=jnp.float32,
            )
        out_ref[...] = (base_ref[...].astype(jnp.float32) + update).astype(out_ref.dtype)

    in_specs = [pl.BlockSpec((near * depth, tile), lambda i, m: (0, i))] * groups + [ANY] * groups + [slab]
    operands = [*lefts, *rights, base]
    aliases = {}
    if out is not None:
        in_specs.append(ANY)
        operands.append(out)
        aliases = {len(operands): 0}
    return pl.pallas_call(
        kernel,
        grid_spec=pltpu.PrefetchScalarGridSpec(
            num_scalar_prefetch=1,
            grid=(rows // tile,),
            in_specs=in_specs,
            out_specs=slab,
            scratch_shapes=[pltpu.VMEM((n, depth, w), base.dtype), pltpu.SemaphoreType.DMA((n,))],
        ),
        out_shape=jax.ShapeDtypeStruct(base.shape, base.dtype),
        input_output_aliases=aliases,
        compiler_params=pltpu.CompilerParams(vmem_limit_bytes=VMEM),
        cost_estimate=NO_COST,
        name="merge",
    )(me.reshape(1), *operands)


def local(n, base_slab, down_factors, up_factors, mix_coeffs):
    depth, rows = down_factors.shape
    width = base_slab.shape[1]
    quads, half = n // 4, n // 2
    me = lax.axis_index("col").astype(jnp.int32)

    def swap(v, bit):
        return lax.ppermute(v, "col", [(i, i ^ bit) for i in range(n)])

    def scale(block, source):
        owners = (source * depth + jnp.arange(depth, dtype=jnp.int32)) // RANK
        matches = owners[:, None] == jnp.arange(mix_coeffs.shape[0], dtype=jnp.int32)[None, :]
        per_rank = jnp.sum(jnp.where(matches, mix_coeffs[None, :], 0.0), axis=1)
        return (block.astype(jnp.float32) * per_rank[:, None]).astype(jnp.bfloat16)

    far = swap(down_factors, half)
    held = {0: scale(down_factors, me)}
    bit = half // 2
    while bit >= 4:
        for k in list(held):
            held[k ^ bit] = swap(held[k], bit)
        bit //= 2

    fours = [list(range(i, i + 4)) for i in range(0, n, 4)]

    def gather(v):
        return lax.all_gather(v, "col", axis_index_groups=fours, axis=0, tiled=True)

    spans = chunk_spans(width)
    last = len(spans) - 1
    w0 = spans[0][1]
    put = functools.partial(assemble, me=me, depth=depth, width=width)

    def for_core(offset, w, after):
        plan = [("own", 4 * dz + 2 * dx + 1) for dx in range(2) for dz in range(quads)]
        return put([plan], {"up": up_factors}, offset=offset, w=w, after=after)[0]

    def for_x(q, after=()):
        offset, w = spans[q]
        at = offset - w0
        plan = [b for dz in range(quads) for b in (("own", 4 * dz + 2), ("core", quads + dz, at))]
        return put([plan], {"up": up_factors, "core": got_c}, offset=offset, w=w, after=after)[0]

    def for_z(q, got_x):
        offset, w = spans[q]
        at = offset - w0
        plan = [
            [("own", 4 * dz), ("core", dz, at), ("x", 2 * dz, 0), ("x", 2 * dz + 1, 0)]
            for dz in range(quads)
        ]
        return put(plan, {"up": up_factors, "core": got_c, "x": got_x}, offset=offset, w=w)

    plan = [[("own", 4 * dz + j) for dz in range(quads)] for j in range(1, 4)]
    to_near = put(plan, {"up": up_factors}, offset=0, w=w0)
    near = [swap(v, j) for j, v in zip((1, 2, 3), to_near)]
    to_x = None
    if last:
        got_c = swap(for_core(w0, width - w0, to_near[:1]), 1)
        to_x = for_x(1)
    plan = [[("own", 4 * dz)] + [(j, dz, 0) for j in range(3)] for dz in range(quads)]
    to_z = put(plan, {"up": up_factors, **dict(enumerate(near))}, offset=0, w=w0)

    out, lefts, panels, merged = None, None, [], 0
    for q in range(last + 1):
        to_z, to_x, panels, out = lax.optimization_barrier((to_z, to_x, panels, out))
        if q == 0:
            held, far, to_z = lax.optimization_barrier((held, far, to_z))
            held[half] = scale(far, me ^ half)
            bit = half // 2
            while bit >= 4:
                for k in list(held):
                    if k >= half and k ^ bit not in held:
                        held[k ^ bit] = swap(held[k], bit)
                bit //= 2
            lefts = [gather(held[4 * dz]) for dz in range(quads)]
        if q == 2:
            lefts, panels = lax.optimization_barrier((lefts, panels))
        here = [swap(v, 4 * dz) if dz else v for dz, v in enumerate(to_z)]
        if q < last:
            got_x = swap(to_x, 2)
            to_z = for_z(q + 1, got_x)
            if q + 1 < last:
                to_x = for_x(q + 2)
        while q >= 2 and merged < q:
            out = merge(lefts, panels[merged], me, base_slab, out, *spans[merged])
            merged += 1
        panels = panels + [here]
    while merged <= last:
        out = merge(lefts, panels[merged], me, base_slab, out, *spans[merged])
        merged += 1
    return out


def solution(mesh):
    in_specs = (
        P("groups", "col"),
        P(("groups", "col"), None),
        P(("groups", "col"), None),
        P("groups"),
    )
    out_specs = P("groups", "col")
    return jax.shard_map(
        functools.partial(local, mesh.shape["col"]),
        mesh=mesh, in_specs=in_specs, out_specs=out_specs, check_vma=False,
    )
```

```python
import functools
import jax
import jax.numpy as jnp
from jax import lax
from jax.experimental import pallas as pl
from jax.experimental.pallas import tpu as pltpu
from jax.sharding import PartitionSpec as P

RANK = 64
UNIT = 256
ORDER = (0, 1, 2, 3, 0, 1, 2, 3, 0, 1, 2, 0, 1)
VMEM = 56 * 1024 * 1024
NO_COST = pl.CostEstimate(flops=1, bytes_accessed=1, transcendentals=0)
ANY = pl.BlockSpec(memory_space=pl.ANY)


def chunk_spans(width):
    units = width // UNIT
    if width % UNIT or units < 8:
        return [(0, width)]
    sizes = [0, 0, 0, 0]
    for i in range(units):
        sizes[ORDER[i % len(ORDER)]] += UNIT
    return [(sum(sizes[:i]), s) for i, s in enumerate(sizes)]


def assemble(plan, sources, me, depth, width):
    up = sources["up"]
    if width % 128:
        outs = []
        for offset, w, blocks in plan:
            parts = []
            for b in blocks:
                if b[0] == "own":
                    parts.append(lax.dynamic_slice(up, (0, (me ^ b[1]) * width + offset), (depth, w)))
                else:
                    parts.append(sources[b[0]][b[1]][:, b[2] : b[2] + w])
            outs.append(jnp.stack(parts))
        return outs
    tile = 32 if depth % 32 == 0 else depth
    el = pl.Element
    in_specs, operands = [], []
    for offset, w, blocks in plan:
        for b in blocks:
            if b[0] == "own":
                in_specs.append(pl.BlockSpec(
                    (el(tile), el(w)),
                    lambda i, m, r=b[1], offset=offset: (
                        i * tile, pl.multiple_of((m[0] ^ r) * width + offset, 128))))
                operands.append(up)
            else:
                in_specs.append(pl.BlockSpec(
                    (el(1), el(tile), el(w)), lambda i, m, lead=b[1], at=b[2]: (lead, i * tile, at)))
                operands.append(sources[b[0]])

    def kernel(m, *refs):
        ins, outs = refs[: len(operands)], refs[len(operands) :]
        k = 0
        for (_, w, blocks), out in zip(plan, outs):
            for j in range(len(blocks)):
                out[j] = ins[k][...].reshape(tile, w)
                k += 1

    return pl.pallas_call(
        kernel,
        grid_spec=pltpu.PrefetchScalarGridSpec(
            num_scalar_prefetch=1,
            grid=(depth // tile,),
            in_specs=in_specs,
            out_specs=[pl.BlockSpec((len(blocks), tile, w), lambda i, m: (0, i, 0)) for _, w, blocks in plan],
        ),
        out_shape=[jax.ShapeDtypeStruct((len(blocks), depth, w), up.dtype) for _, w, blocks in plan],
        compiler_params=pltpu.CompilerParams(vmem_limit_bytes=VMEM),
        cost_estimate=NO_COST,
        name="assemble",
    )(me.reshape(1), *operands)


def merge(lefts, rights, me, base, out, offset, w):
    rows, width = base.shape
    depth = rights[0].shape[1]
    tile, near, groups = 512, rights[0].shape[0], len(lefts)
    n = near * groups
    if w == width:
        slab = pl.BlockSpec((tile, w), lambda i, m: (i, 0))
    else:
        slab = pl.BlockSpec((pl.Element(tile), pl.Element(w)), lambda i, m: (i * tile, offset))

    def kernel(m, *refs):
        left, right = refs[:groups], refs[groups : 2 * groups]
        base_ref, (out_ref, panel, sem) = refs[2 * groups], refs[-3:]

        @pl.when(pl.program_id(0) == 0)
        def _():
            copies = []
            for g in range(groups):
                for j in range(near):
                    place = g * near + (m[0] ^ j) % near
                    copies.append(pltpu.make_async_copy(right[g].at[j], panel.at[place], sem.at[g * near + j]))
            for c in copies:
                c.start()
            for c in copies:
                c.wait()

        update = 0.0
        for g in range(groups):
            update += lax.dot_general(
                left[g][...],
                panel[g * near : (g + 1) * near].reshape(near * depth, w),
                (((0,), (0,)), ((), ())),
                preferred_element_type=jnp.float32,
            )
        out_ref[...] = (base_ref[...].astype(jnp.float32) + update).astype(out_ref.dtype)

    in_specs = [pl.BlockSpec((near * depth, tile), lambda i, m: (0, i))] * groups + [ANY] * groups + [slab]
    operands = [*lefts, *rights, base]
    aliases = {}
    if out is not None:
        in_specs.append(ANY)
        operands.append(out)
        aliases = {len(operands): 0}
    return pl.pallas_call(
        kernel,
        grid_spec=pltpu.PrefetchScalarGridSpec(
            num_scalar_prefetch=1,
            grid=(rows // tile,),
            in_specs=in_specs,
            out_specs=slab,
            scratch_shapes=[pltpu.VMEM((n, depth, w), base.dtype), pltpu.SemaphoreType.DMA((n,))],
        ),
        out_shape=jax.ShapeDtypeStruct(base.shape, base.dtype),
        input_output_aliases=aliases,
        compiler_params=pltpu.CompilerParams(vmem_limit_bytes=VMEM),
        cost_estimate=NO_COST,
        name="merge",
    )(me.reshape(1), *operands)


def local(n, base_slab, down_factors, up_factors, mix_coeffs):
    depth, rows = down_factors.shape
    width = base_slab.shape[1]
    quads, half = n // 4, n // 2
    me = lax.axis_index("col").astype(jnp.int32)

    def swap(v, bit):
        return lax.ppermute(v, "col", [(i, i ^ bit) for i in range(n)])

    owners = (me * depth + jnp.arange(depth, dtype=jnp.int32)) // RANK
    matches = owners[:, None] == jnp.arange(mix_coeffs.shape[0], dtype=jnp.int32)[None, :]
    per_rank = jnp.sum(jnp.where(matches, mix_coeffs[None, :], 0.0), axis=1)
    scaled = (down_factors.astype(jnp.float32) * per_rank[:, None]).astype(jnp.bfloat16)

    def across(v, at):
        got, bit = {at: v}, half // 2
        while bit >= 4:
            got.update({k ^ bit: swap(b, bit) for k, b in list(got.items())})
            bit //= 2
        return got

    far = swap(scaled, half)
    held = across(scaled, 0)
    fours = [list(range(i, i + 4)) for i in range(0, n, 4)]

    def gather(v):
        return lax.all_gather(v, "col", axis_index_groups=fours, axis=0, tiled=True)

    spans = chunk_spans(width)
    last = len(spans) - 1
    w0 = spans[0][1]
    put = functools.partial(assemble, me=me, depth=depth, width=width)

    to_core = [("own", 4 * dz + 2 * dx + 1) for dx in range(2) for dz in range(quads)]
    to_2, to_3, to_1 = put(
        [(0, w0, [("own", 4 * dz + j) for dz in range(quads)]) for j in (2, 3)] + [(0, width, to_core)],
        {"up": up_factors},
    )
    got_2, got_3, got_c = swap(to_2, 2), swap(to_3, 3), swap(to_1, 1)
    src = {"up": up_factors, "core": got_c, 2: got_2, 3: got_3}

    def for_x(q):
        offset, w = spans[q]
        plan = [b for dz in range(quads) for b in (("own", 4 * dz + 2), ("core", quads + dz, offset))]
        return put([(offset, w, plan)], src)[0]

    def for_z(q, got_x):
        offset, w = spans[q]
        return put([
            (offset, w, [("own", 4 * dz), ("core", dz, offset), ("x", 2 * dz, 0), ("x", 2 * dz + 1, 0)])
            for dz in range(quads)
        ], {**src, "x": got_x})

    to_x = for_x(1) if last else None
    to_z = put([
        (0, w0, [("own", 4 * dz), ("core", dz, 0), (2, dz, 0), (3, dz, 0)]) for dz in range(quads)
    ], src)

    out, panels, merged = None, [], 0
    far, held, to_z, to_x = lax.optimization_barrier((far, held, to_z, to_x))
    lefts = {k: gather(v) for k, v in held.items()}
    lefts[half] = gather(far)
    far_held = across(far, half)
    for q in range(last + 1):
        if q:
            to_z, to_x, panels, out = lax.optimization_barrier((to_z, to_x, panels, out))
        if q == min(1, last):
            far_held, to_z, panels = lax.optimization_barrier((far_held, to_z, panels))
            lefts.update({k: gather(v) for k, v in far_held.items() if k != half})
        here = [swap(v, 4 * dz) if dz else v for dz, v in enumerate(to_z)]
        if q < last:
            got_x = swap(to_x, 2)
            to_z = for_z(q + 1, got_x)
            if q + 1 < last:
                to_x = for_x(q + 2)
        if q == min(2, last):
            lefts, panels = lax.optimization_barrier((lefts, panels))
            left = [lefts[4 * dz] for dz in range(quads)]
        panels = panels + [here]
        while merged < (q if q >= 2 and q < last else q + 1 if q == last else 0):
            out = merge(left, panels[merged], me, base_slab, out, *spans[merged])
            merged += 1
    return out


def solution(mesh):
    in_specs = (
        P("groups", "col"),
        P(("groups", "col"), None),
        P(("groups", "col"), None),
        P("groups"),
    )
    out_specs = P("groups", "col")
    return jax.shard_map(
        functools.partial(local, mesh.shape["col"]),
        mesh=mesh, in_specs=in_specs, out_specs=out_specs, check_vma=False,
    )
```

```python
import functools
import jax
import jax.numpy as jnp
from jax import lax
from jax.experimental import pallas as pl
from jax.experimental.pallas import tpu as pltpu
from jax.sharding import PartitionSpec as P

RANK = 64
UNIT = 128
TILE = 1024
SHARES = (7, 8, 8, 3)
VMEM = 56 * 1024 * 1024
NO_COST = pl.CostEstimate(flops=1, bytes_accessed=1, transcendentals=0)
ANY = pl.BlockSpec(memory_space=pl.ANY)


def chunk_spans(width):
    units = width // UNIT
    if width % UNIT or units < sum(SHARES):
        return [(0, width)]
    ends = [units * sum(SHARES[: i + 1]) // sum(SHARES) * UNIT for i in range(len(SHARES))]
    return [(start, end - start) for start, end in zip([0] + ends, ends)]


def assemble(plan, sources, me, depth, width):
    up = sources["up"]
    if width % 128:
        outs = []
        for offset, w, blocks in plan:
            parts = []
            for b in blocks:
                if b[0] == "own":
                    parts.append(lax.dynamic_slice(up, (0, (me ^ b[1]) * width + offset), (depth, w)))
                else:
                    parts.append(sources[b[0]][b[1]][:, b[2] : b[2] + w])
            outs.append(jnp.stack(parts))
        return outs
    tile = 32 if depth % 32 == 0 else depth
    el = pl.Element
    in_specs, operands = [], []
    for offset, w, blocks in plan:
        for b in blocks:
            if b[0] == "own":
                in_specs.append(pl.BlockSpec(
                    (el(tile), el(w)),
                    lambda i, m, r=b[1], offset=offset: (
                        i * tile, pl.multiple_of((m[0] ^ r) * width + offset, 128))))
                operands.append(up)
            else:
                in_specs.append(pl.BlockSpec(
                    (el(1), el(tile), el(w)), lambda i, m, lead=b[1], at=b[2]: (lead, i * tile, at)))
                operands.append(sources[b[0]])

    def kernel(m, *refs):
        ins, outs = refs[: len(operands)], refs[len(operands) :]
        k = 0
        for (_, w, blocks), out in zip(plan, outs):
            for j in range(len(blocks)):
                out[j] = ins[k][...].reshape(tile, w)
                k += 1

    return pl.pallas_call(
        kernel,
        grid_spec=pltpu.PrefetchScalarGridSpec(
            num_scalar_prefetch=1,
            grid=(depth // tile,),
            in_specs=in_specs,
            out_specs=[pl.BlockSpec((len(blocks), tile, w), lambda i, m: (0, i, 0)) for _, w, blocks in plan],
        ),
        out_shape=[jax.ShapeDtypeStruct((len(blocks), depth, w), up.dtype) for _, w, blocks in plan],
        compiler_params=pltpu.CompilerParams(vmem_limit_bytes=VMEM),
        cost_estimate=NO_COST,
        name="assemble",
    )(me.reshape(1), *operands)


def merge(lefts, rights, me, base, out, offset, w):
    rows, width = base.shape
    near, depth, _ = rights[0].shape
    groups, tile = len(lefts), TILE
    if w == width:
        slab = pl.BlockSpec((tile, w), lambda i, m: (i, 0))
    else:
        slab = pl.BlockSpec((pl.Element(tile), pl.Element(w)), lambda i, m: (i * tile, offset))

    def kernel(m, *refs):
        left, right = refs[:groups], refs[groups : groups * (1 + near)]
        base_ref, out_ref = refs[groups * (1 + near)], refs[-1]
        update = 0.0
        for g in range(groups):
            panel = jnp.concatenate([r[0] for r in right[g * near : (g + 1) * near]], axis=0)
            update += lax.dot_general(
                left[g][...], panel, (((0,), (0,)), ((), ())), preferred_element_type=jnp.float32
            )
        out_ref[...] = (base_ref[...].astype(jnp.float32) + update).astype(out_ref.dtype)

    blocks = [
        pl.BlockSpec((1, depth, w), lambda i, m, j=j: ((m[0] ^ j) % near, 0, 0)) for j in range(near)
    ]
    in_specs = [pl.BlockSpec((near * depth, tile), lambda i, m: (0, i))] * groups + blocks * groups + [slab]
    operands = [*lefts, *[r for r in rights for _ in range(near)], base]
    aliases = {}
    if out is not None:
        in_specs.append(ANY)
        operands.append(out)
        aliases = {len(operands): 0}
    return pl.pallas_call(
        kernel,
        grid_spec=pltpu.PrefetchScalarGridSpec(
            num_scalar_prefetch=1, grid=(rows // tile,), in_specs=in_specs, out_specs=slab
        ),
        out_shape=jax.ShapeDtypeStruct(base.shape, base.dtype),
        input_output_aliases=aliases,
        compiler_params=pltpu.CompilerParams(vmem_limit_bytes=VMEM),
        cost_estimate=NO_COST,
        name="merge",
    )(me.reshape(1), *operands)


def local(n, base_slab, down_factors, up_factors, mix_coeffs):
    depth, rows = down_factors.shape
    width = base_slab.shape[1]
    quads, half = n // 4, n // 2
    me = lax.axis_index("col").astype(jnp.int32)

    def swap(v, bit):
        return lax.ppermute(v, "col", [(i, i ^ bit) for i in range(n)])

    owners = (me * depth + jnp.arange(depth, dtype=jnp.int32)) // RANK
    matches = owners[:, None] == jnp.arange(mix_coeffs.shape[0], dtype=jnp.int32)[None, :]
    per_rank = jnp.sum(jnp.where(matches, mix_coeffs[None, :], 0.0), axis=1)
    scaled = (down_factors.astype(jnp.float32) * per_rank[:, None]).astype(jnp.bfloat16)

    def across(v, at):
        got, bit = {at: v}, half // 2
        while bit >= 4:
            got.update({k ^ bit: swap(b, bit) for k, b in list(got.items())})
            bit //= 2
        return got

    far = swap(scaled, half)
    held = across(scaled, 0)
    fours = [list(range(i, i + 4)) for i in range(0, n, 4)]

    def gather(v):
        return lax.all_gather(v, "col", axis_index_groups=fours, axis=0, tiled=True)

    spans = chunk_spans(width)
    last = len(spans) - 1
    w0 = spans[0][1]
    put = functools.partial(assemble, me=me, depth=depth, width=width)

    to_core = [("own", 4 * dz + 2 * dx + 1) for dx in range(2) for dz in range(quads)]
    to_2, to_3 = put(
        [(0, w0, [("own", 4 * dz + j) for dz in range(quads)]) for j in (2, 3)], {"up": up_factors}
    )
    to_1 = put([(0, width, to_core)], {"up": up_factors})[0]
    got_2, got_3, got_c = swap(to_2, 2), swap(to_3, 3), swap(to_1, 1)
    src = {"up": up_factors, "core": got_c, 2: got_2, 3: got_3}

    def for_x(q):
        offset, w = spans[q]
        plan = [b for dz in range(quads) for b in (("own", 4 * dz + 2), ("core", quads + dz, offset))]
        return put([(offset, w, plan)], src)[0]

    def for_z(q, got_x):
        offset, w = spans[q]
        return put([
            (offset, w, [("own", 4 * dz), ("core", dz, offset), ("x", 2 * dz, 0), ("x", 2 * dz + 1, 0)])
            for dz in range(quads)
        ], {**src, "x": got_x})

    far, held, got_2, got_3 = lax.optimization_barrier((far, held, got_2, got_3))
    lefts = {half: gather(far)}
    src.update({2: got_2, 3: got_3})
    to_x = for_x(1) if last else None
    to_z = put([
        (0, w0, [("own", 4 * dz), ("core", dz, 0), (2, dz, 0), (3, dz, 0)]) for dz in range(quads)
    ], src)

    out, panels, merged = None, [], 0
    far, held, to_z, to_x = lax.optimization_barrier((far, held, to_z, to_x))
    lefts.update({k: gather(v) for k, v in held.items()})
    far_held = across(far, half)
    for q in range(last + 1):
        if q:
            to_z, to_x, panels, out = lax.optimization_barrier((to_z, to_x, panels, out))
        if q == min(1, last):
            far_held, to_z, panels = lax.optimization_barrier((far_held, to_z, panels))
            lefts.update({k: gather(v) for k, v in far_held.items() if k != half})
        here = [swap(v, 4 * dz) if dz else v for dz, v in enumerate(to_z)]
        if q < last:
            got_x = swap(to_x, 2)
            to_z = for_z(q + 1, got_x)
            if q + 1 < last:
                to_x = for_x(q + 2)
        if q == min(2, last):
            lefts, panels = lax.optimization_barrier((lefts, panels))
            left = [lefts[4 * dz] for dz in range(quads)]
        panels = panels + [here]
        while merged < (q if q >= 2 and q < last else q + 1 if q == last else 0):
            out = merge(left, panels[merged], me, base_slab, out, *spans[merged])
            merged += 1
    return out


def solution(mesh):
    in_specs = (
        P("groups", "col"),
        P(("groups", "col"), None),
        P(("groups", "col"), None),
        P("groups"),
    )
    out_specs = P("groups", "col")
    return jax.shard_map(
        functools.partial(local, mesh.shape["col"]),
        mesh=mesh, in_specs=in_specs, out_specs=out_specs, check_vma=False,
    )
```

```python
import functools
import jax
import jax.numpy as jnp
from jax import lax
from jax.experimental import pallas as pl
from jax.experimental.pallas import tpu as pltpu
from jax.sharding import PartitionSpec as P

RANK = 64
UNIT = 128
TILE = 1024
SHARES = (7, 8, 8, 3)
VMEM = 56 * 1024 * 1024
NO_COST = pl.CostEstimate(flops=1, bytes_accessed=1, transcendentals=0)
ANY = pl.BlockSpec(memory_space=pl.ANY)


def chunk_spans(width):
    units = width // UNIT
    if width % UNIT or units < sum(SHARES):
        return [(0, width)]
    ends = [units * sum(SHARES[: i + 1]) // sum(SHARES) * UNIT for i in range(len(SHARES))]
    return [(start, end - start) for start, end in zip([0] + ends, ends)]


def assemble(plan, sources, me, depth, width):
    up = sources["up"]
    if width % 128:
        outs = []
        for offset, w, blocks in plan:
            parts = []
            for b in blocks:
                if b[0] == "own":
                    parts.append(lax.dynamic_slice(up, (0, (me ^ b[1]) * width + offset), (depth, w)))
                else:
                    parts.append(sources[b[0]][b[1]][:, b[2] : b[2] + w])
            outs.append(jnp.stack(parts))
        return outs
    tile = 64 if depth % 64 == 0 else depth
    el = pl.Element
    in_specs, operands = [], []
    for offset, w, blocks in plan:
        for b in blocks:
            if b[0] == "own":
                in_specs.append(pl.BlockSpec(
                    (el(tile), el(w)),
                    lambda i, m, r=b[1], offset=offset: (
                        i * tile, pl.multiple_of((m[0] ^ r) * width + offset, 128))))
                operands.append(up)
            else:
                in_specs.append(pl.BlockSpec(
                    (el(1), el(tile), el(w)), lambda i, m, lead=b[1], at=b[2]: (lead, i * tile, at)))
                operands.append(sources[b[0]])

    def kernel(m, *refs):
        ins, outs = refs[: len(operands)], refs[len(operands) :]
        k = 0
        for (_, w, blocks), out in zip(plan, outs):
            for j in range(len(blocks)):
                out[j] = ins[k][...].reshape(tile, w)
                k += 1

    return pl.pallas_call(
        kernel,
        grid_spec=pltpu.PrefetchScalarGridSpec(
            num_scalar_prefetch=1,
            grid=(depth // tile,),
            in_specs=in_specs,
            out_specs=[pl.BlockSpec((len(blocks), tile, w), lambda i, m: (0, i, 0)) for _, w, blocks in plan],
        ),
        out_shape=[jax.ShapeDtypeStruct((len(blocks), depth, w), up.dtype) for _, w, blocks in plan],
        compiler_params=pltpu.CompilerParams(vmem_limit_bytes=VMEM),
        cost_estimate=NO_COST,
        name="assemble",
    )(me.reshape(1), *operands)


def merge(lefts, rights, me, base, out, offset, w):
    rows, width = base.shape
    near, depth, _ = rights[0].shape
    groups, tile = len(lefts), TILE
    if w == width:
        slab = pl.BlockSpec((tile, w), lambda i, m: (i, 0))
    else:
        slab = pl.BlockSpec((pl.Element(tile), pl.Element(w)), lambda i, m: (i * tile, offset))

    def kernel(m, *refs):
        left, right = refs[:groups], refs[groups : groups * (1 + near)]
        base_ref, out_ref = refs[groups * (1 + near)], refs[-1]
        update = 0.0
        for g in range(groups):
            panel = jnp.concatenate([r[0] for r in right[g * near : (g + 1) * near]], axis=0)
            update += lax.dot_general(
                left[g][...], panel, (((0,), (0,)), ((), ())), preferred_element_type=jnp.float32
            )
        out_ref[...] = (base_ref[...].astype(jnp.float32) + update).astype(out_ref.dtype)

    blocks = [
        pl.BlockSpec((1, depth, w), lambda i, m, j=j: ((m[0] ^ j) % near, 0, 0)) for j in range(near)
    ]
    in_specs = [pl.BlockSpec((near * depth, tile), lambda i, m: (0, i))] * groups + blocks * groups + [slab]
    operands = [*lefts, *[r for r in rights for _ in range(near)], base]
    aliases = {}
    if out is not None:
        in_specs.append(ANY)
        operands.append(out)
        aliases = {len(operands): 0}
    return pl.pallas_call(
        kernel,
        grid_spec=pltpu.PrefetchScalarGridSpec(
            num_scalar_prefetch=1, grid=(rows // tile,), in_specs=in_specs, out_specs=slab
        ),
        out_shape=jax.ShapeDtypeStruct(base.shape, base.dtype),
        input_output_aliases=aliases,
        compiler_params=pltpu.CompilerParams(vmem_limit_bytes=VMEM),
        cost_estimate=NO_COST,
        name="merge",
    )(me.reshape(1), *operands)


def local(n, base_slab, down_factors, up_factors, mix_coeffs):
    depth, rows = down_factors.shape
    width = base_slab.shape[1]
    quads, half = n // 4, n // 2
    me = lax.axis_index("col").astype(jnp.int32)

    def swap(v, bit):
        return lax.ppermute(v, "col", [(i, i ^ bit) for i in range(n)])

    owners = (me * depth + jnp.arange(depth, dtype=jnp.int32)) // RANK
    matches = owners[:, None] == jnp.arange(mix_coeffs.shape[0], dtype=jnp.int32)[None, :]
    per_rank = jnp.sum(jnp.where(matches, mix_coeffs[None, :], 0.0), axis=1)
    scaled = (down_factors.astype(jnp.float32) * per_rank[:, None]).astype(jnp.bfloat16)

    def across(v, at):
        got, bit = {at: v}, half // 2
        while bit >= 4:
            got.update({k ^ bit: swap(b, bit) for k, b in list(got.items())})
            bit //= 2
        return got

    far = swap(scaled, half)
    held = across(scaled, 0)
    fours = [list(range(i, i + 4)) for i in range(0, n, 4)]

    def gather(v):
        return lax.all_gather(v, "col", axis_index_groups=fours, axis=0, tiled=True)

    spans = chunk_spans(width)
    last = len(spans) - 1
    w0 = spans[0][1]
    put = functools.partial(assemble, me=me, depth=depth, width=width)

    to_core = [("own", 4 * dz + 2 * dx + 1) for dx in range(2) for dz in range(quads)]
    to_2, to_3 = put(
        [(0, w0, [("own", 4 * dz + j) for dz in range(quads)]) for j in (2, 3)], {"up": up_factors}
    )
    to_1 = put([(0, width, to_core)], {"up": up_factors})[0]
    got_2, got_3, got_c = swap(to_2, 2), swap(to_3, 3), swap(to_1, 1)
    src = {"up": up_factors, "core": got_c, 2: got_2, 3: got_3}

    def x_plan(q):
        offset, w = spans[q]
        return (offset, w, [
            b for dz in range(quads) for b in (("own", 4 * dz + 2), ("core", quads + dz, offset))])

    def for_z(q, got_x):
        offset, w = spans[q]
        return put([
            (offset, w, [("own", 4 * dz), ("core", dz, offset), ("x", 2 * dz, 0), ("x", 2 * dz + 1, 0)])
            for dz in range(quads)
        ], {**src, "x": got_x})

    far, held, got_2, got_3 = lax.optimization_barrier((far, held, got_2, got_3))
    lefts = {half: gather(far)}
    src.update({2: got_2, 3: got_3})
    to_z = put(
        [(0, w0, [("own", 4 * dz), ("core", dz, 0), (2, dz, 0), (3, dz, 0)]) for dz in range(quads)]
        + ([x_plan(1)] if last else []),
        src,
    )
    to_z, to_x = to_z[:quads], to_z[quads:]

    out, panels, merged = None, [], 0
    far, held, to_z, to_x = lax.optimization_barrier((far, held, to_z, to_x))
    lefts.update({k: gather(v) for k, v in held.items()})
    far_held = across(far, half)
    for q in range(last + 1):
        if q:
            to_z, to_x, panels, out = lax.optimization_barrier((to_z, to_x, panels, out))
        if q == min(1, last):
            far_held, to_z, panels = lax.optimization_barrier((far_held, to_z, panels))
            lefts.update({k: gather(v) for k, v in far_held.items() if k != half})
        here = [swap(v, 4 * dz) if dz else v for dz, v in enumerate(to_z)]
        if q < last:
            got_x = swap(to_x[0], 2)
            to_z = for_z(q + 1, got_x)
            if q + 1 < last:
                to_x = put([x_plan(q + 2)], src)
        if q == min(2, last):
            lefts, panels = lax.optimization_barrier((lefts, panels))
            left = [lefts[4 * dz] for dz in range(quads)]
        panels = panels + [here]
        while merged < (q if q >= 2 and q < last else q + 1 if q == last else 0):
            out = merge(left, panels[merged], me, base_slab, out, *spans[merged])
            merged += 1
    return out


def solution(mesh):
    in_specs = (
        P("groups", "col"),
        P(("groups", "col"), None),
        P(("groups", "col"), None),
        P("groups"),
    )
    out_specs = P("groups", "col")
    return jax.shard_map(
        functools.partial(local, mesh.shape["col"]),
        mesh=mesh, in_specs=in_specs, out_specs=out_specs, check_vma=False,
    )
```

```python
import functools
import jax
import jax.numpy as jnp
from jax import lax
from jax.experimental import pallas as pl
from jax.experimental.pallas import tpu as pltpu
from jax.sharding import PartitionSpec as P

RANK = 64
UNIT = 128
TILE = 1024
SHARES = (7, 8, 6, 3, 2)
VMEM = 56 * 1024 * 1024
NO_COST = pl.CostEstimate(flops=1, bytes_accessed=1, transcendentals=0)
ANY = pl.BlockSpec(memory_space=pl.ANY)


def chunk_spans(width):
    units = width // UNIT
    if width % UNIT or units < sum(SHARES):
        return [(0, width)]
    ends = [units * sum(SHARES[: i + 1]) // sum(SHARES) * UNIT for i in range(len(SHARES))]
    return [(start, end - start) for start, end in zip([0] + ends, ends)]


def assemble(plan, sources, me, depth, width):
    up = sources["up"]
    if width % 128:
        outs = []
        for offset, w, blocks in plan:
            parts = []
            for b in blocks:
                if b[0] == "own":
                    parts.append(lax.dynamic_slice(up, (0, (me ^ b[1]) * width + offset), (depth, w)))
                else:
                    parts.append(sources[b[0]][b[1]][:, b[2] : b[2] + w])
            outs.append(jnp.stack(parts))
        return outs
    tile = 64 if depth % 64 == 0 else depth
    el = pl.Element
    in_specs, operands = [], []
    for offset, w, blocks in plan:
        for b in blocks:
            if b[0] == "own":
                in_specs.append(pl.BlockSpec(
                    (el(tile), el(w)),
                    lambda i, m, r=b[1], offset=offset: (
                        i * tile, pl.multiple_of((m[0] ^ r) * width + offset, 128))))
                operands.append(up)
            else:
                in_specs.append(pl.BlockSpec(
                    (el(1), el(tile), el(w)), lambda i, m, lead=b[1], at=b[2]: (lead, i * tile, at)))
                operands.append(sources[b[0]])

    def kernel(m, *refs):
        ins, outs = refs[: len(operands)], refs[len(operands) :]
        k = 0
        for (_, w, blocks), out in zip(plan, outs):
            for j in range(len(blocks)):
                out[j] = ins[k][...].reshape(tile, w)
                k += 1

    return pl.pallas_call(
        kernel,
        grid_spec=pltpu.PrefetchScalarGridSpec(
            num_scalar_prefetch=1,
            grid=(depth // tile,),
            in_specs=in_specs,
            out_specs=[pl.BlockSpec((len(blocks), tile, w), lambda i, m: (0, i, 0)) for _, w, blocks in plan],
        ),
        out_shape=[jax.ShapeDtypeStruct((len(blocks), depth, w), up.dtype) for _, w, blocks in plan],
        compiler_params=pltpu.CompilerParams(vmem_limit_bytes=VMEM),
        cost_estimate=NO_COST,
        name="assemble",
    )(me.reshape(1), *operands)


def merge(lefts, rights, me, base, out, offset, w):
    rows, width = base.shape
    near, depth, _ = rights[0].shape
    groups, tile = len(lefts), TILE
    if w == width:
        slab = pl.BlockSpec((tile, w), lambda i, m: (i, 0))
    else:
        slab = pl.BlockSpec((pl.Element(tile), pl.Element(w)), lambda i, m: (i * tile, offset))

    def kernel(m, *refs):
        left, right = refs[:groups], refs[groups : groups * (1 + near)]
        base_ref, out_ref = refs[groups * (1 + near)], refs[-1]
        update = 0.0
        for g in range(groups):
            panel = jnp.concatenate([r[0] for r in right[g * near : (g + 1) * near]], axis=0)
            update += lax.dot_general(
                left[g][...], panel, (((0,), (0,)), ((), ())), preferred_element_type=jnp.float32
            )
        out_ref[...] = (base_ref[...].astype(jnp.float32) + update).astype(out_ref.dtype)

    blocks = [
        pl.BlockSpec((1, depth, w), lambda i, m, j=j: ((m[0] ^ j) % near, 0, 0)) for j in range(near)
    ]
    in_specs = [pl.BlockSpec((near * depth, tile), lambda i, m: (0, i))] * groups + blocks * groups + [slab]
    operands = [*lefts, *[r for r in rights for _ in range(near)], base]
    aliases = {}
    if out is not None:
        in_specs.append(ANY)
        operands.append(out)
        aliases = {len(operands): 0}
    return pl.pallas_call(
        kernel,
        grid_spec=pltpu.PrefetchScalarGridSpec(
            num_scalar_prefetch=1, grid=(rows // tile,), in_specs=in_specs, out_specs=slab
        ),
        out_shape=jax.ShapeDtypeStruct(base.shape, base.dtype),
        input_output_aliases=aliases,
        compiler_params=pltpu.CompilerParams(vmem_limit_bytes=VMEM),
        cost_estimate=NO_COST,
        name="merge",
    )(me.reshape(1), *operands)


def local(n, base_slab, down_factors, up_factors, mix_coeffs):
    depth, rows = down_factors.shape
    width = base_slab.shape[1]
    quads, half = n // 4, n // 2
    me = lax.axis_index("col").astype(jnp.int32)

    def swap(v, bit):
        return lax.ppermute(v, "col", [(i, i ^ bit) for i in range(n)])

    owners = (me * depth + jnp.arange(depth, dtype=jnp.int32)) // RANK
    matches = owners[:, None] == jnp.arange(mix_coeffs.shape[0], dtype=jnp.int32)[None, :]
    per_rank = jnp.sum(jnp.where(matches, mix_coeffs[None, :], 0.0), axis=1)
    scaled = (down_factors.astype(jnp.float32) * per_rank[:, None]).astype(jnp.bfloat16)

    def across(v, at):
        got, bit = {at: v}, half // 2
        while bit >= 4:
            got.update({k ^ bit: swap(b, bit) for k, b in list(got.items())})
            bit //= 2
        return got

    far = swap(scaled, half)
    held = across(scaled, 0)
    fours = [list(range(i, i + 4)) for i in range(0, n, 4)]

    def gather(v):
        return lax.all_gather(v, "col", axis_index_groups=fours, axis=0, tiled=True)

    spans = chunk_spans(width)
    last = len(spans) - 1
    w0 = spans[0][1]
    put = functools.partial(assemble, me=me, depth=depth, width=width)

    to_core = [("own", 4 * dz + 2 * dx + 1) for dx in range(2) for dz in range(quads)]
    to_2, to_3 = put(
        [(0, w0, [("own", 4 * dz + j) for dz in range(quads)]) for j in (2, 3)], {"up": up_factors}
    )
    to_1 = put([(0, width, to_core)], {"up": up_factors})[0]
    got_2, got_3, got_c = swap(to_2, 2), swap(to_3, 3), swap(to_1, 1)
    src = {"up": up_factors, "core": got_c, 2: got_2, 3: got_3}

    def x_plan(q):
        offset, w = spans[q]
        return (offset, w, [
            b for dz in range(quads) for b in (("own", 4 * dz + 2), ("core", quads + dz, offset))])

    def for_z(q, got_x):
        offset, w = spans[q]
        return put([
            (offset, w, [("own", 4 * dz), ("core", dz, offset), ("x", 2 * dz, 0), ("x", 2 * dz + 1, 0)])
            for dz in range(quads)
        ], {**src, "x": got_x})

    far, held, got_2, got_3 = lax.optimization_barrier((far, held, got_2, got_3))
    lefts = {half: gather(far)}
    src.update({2: got_2, 3: got_3})
    to_z = put(
        [(0, w0, [("own", 4 * dz), ("core", dz, 0), (2, dz, 0), (3, dz, 0)]) for dz in range(quads)]
        + ([x_plan(1)] if last else []),
        src,
    )
    to_z, to_x = to_z[:quads], to_z[quads:]

    out, panels, merged = None, [], 0
    far, held, to_z, to_x = lax.optimization_barrier((far, held, to_z, to_x))
    lefts.update({k: gather(v) for k, v in held.items()})
    far_held = across(far, half)
    for q in range(last + 1):
        if q:
            to_z, to_x, panels, out = lax.optimization_barrier((to_z, to_x, panels, out))
        if q == min(1, last):
            far_held, to_z, panels = lax.optimization_barrier((far_held, to_z, panels))
            lefts.update({k: gather(v) for k, v in far_held.items() if k != half})
        here = [swap(v, 4 * dz) if dz else v for dz, v in enumerate(to_z)]
        if q < last:
            got_x = swap(to_x[0], 2)
            to_z = for_z(q + 1, got_x)
            if q + 1 < last:
                to_x = put([x_plan(q + 2)], src)
        if q == min(2, last):
            lefts, panels = lax.optimization_barrier((lefts, panels))
            left = [lefts[4 * dz] for dz in range(quads)]
        panels = panels + [here]
        while merged < (q if q >= 2 and q < last else q + 1 if q == last else 0):
            out = merge(left, panels[merged], me, base_slab, out, *spans[merged])
            merged += 1
    return out


def solution(mesh):
    in_specs = (
        P("groups", "col"),
        P(("groups", "col"), None),
        P(("groups", "col"), None),
        P("groups"),
    )
    out_specs = P("groups", "col")
    return jax.shard_map(
        functools.partial(local, mesh.shape["col"]),
        mesh=mesh, in_specs=in_specs, out_specs=out_specs, check_vma=False,
    )
```
